1024 devices in a mesh: rep: 64 (over z_hi, x, y), fsdp: 16 (over z_lo, core).
Axes of the slice: x: 4, y: 4, z: 32 (z_hi: 4, z_lo: 8; z = z_hi * 8 + z_lo), core: 2. Of those that a mesh axis runs over, the one named last changes fastest.
Arguments:
- grad_partial: bfloat16 [64, 64, 512, 512], P('rep', 'fsdp'), may hold values from -2 to 2
- owner_block: int32 [64], replicated, may hold values from 0 to 63, each once
- left_stat: float32 [64, 512, 512], P('rep', 'fsdp'), may hold values from -0.1 to 1.6, as said below
- right_stat: float32 [64, 512, 512], P('rep'), may hold values from -0.1 to 1.6, as said below
- left_root: float32 [64, 512, 512], P('rep'), may hold values from -0.05 to 1, as said below
- right_root: float32 [64, 512, 512], P('rep'), may hold values from -0.05 to 1, as said below
Outputs:
- preconditioned: bfloat16 [64, 512, 512], P('rep', 'fsdp')
- left_new: float32 [64, 512, 512], P('rep', 'fsdp')
- right_new: float32 [64, 512, 512], P('rep', 'fsdp')
- left_next: float32 [64, 512, 512], P('rep', 'fsdp')
- right_next: float32 [64, 512, 512], P('rep', 'fsdp')
The draws below stay inside these ranges and needn't reach their ends.
Inputs may be any that keep to these rules, and one draw needn't show every extreme that they name: `owner_block`: every block number appears exactly once. `left_stat`: each slot's matrix is symmetric positive definite. `right_stat`: each slot's matrix is symmetric positive definite. `left_root`: each slot's matrix is symmetric. `right_root`: each slot's matrix is symmetric.
All inputs are finite; a program needn't handle non-finite values.
Results may differ from the reference program's by a relative error of at most 0.0068.
Values may be sent and summed in bfloat16 or wider, within the bound.
No kernel may reach another device: no remote copies, remote signals or barrier semaphores. Data moves between devices by JAX's collectives and lax.ppermute only.
A program may use at most 32 MiB of HBM per device.

```python
import math
import jax
import jax.numpy as jnp
from jax import lax

BS = 512
BLOCKS = 64
N_REP = 64


def symmetric_matrix(noise_draw, diagonal_values, spread):
    mixed_part = (noise_draw + jnp.swapaxes(noise_draw, -1, -2)) * (spread / math.sqrt(2.0))
    identity = jnp.eye(noise_draw.shape[-1], dtype=jnp.float32)
    return mixed_part + identity * diagonal_values[..., None]


def noise_normal(noise_key, full_shape):
    return jnp.clip(jax.random.normal(noise_key, full_shape, jnp.float32), -6.0, 6.0)


def stat_draw(key):
    noise_key, diag_key = jax.random.split(key)
    full_shape = (N_REP, BS, BS)
    noise_draw = noise_normal(noise_key, full_shape)
    diagonal_values = jnp.exp(jax.random.uniform(diag_key, (N_REP, BS), jnp.float32, math.log(0.5), math.log(1.5)))
    return symmetric_matrix(noise_draw, diagonal_values, 0.01)


def root_draw(key):
    noise_key, diag_key = jax.random.split(key)
    full_shape = (N_REP, BS, BS)
    noise_draw = noise_normal(noise_key, full_shape)
    diagonal_values = jax.random.uniform(diag_key, (N_REP, BS), jnp.float32, 0.75, 0.95)
    return symmetric_matrix(noise_draw, diagonal_values, 0.004)


def draw_left_stat(key, part):
    key = jax.random.fold_in(key, 11)
    return stat_draw(key)


def draw_right_stat(key, part):
    key = jax.random.fold_in(key, 12)
    return stat_draw(key)


def draw_left_root(key, part):
    key = jax.random.fold_in(key, 13)
    return root_draw(key)


def draw_right_root(key, part):
    key = jax.random.fold_in(key, 14)
    return root_draw(key)


def shard_levels(own_key, extent, cuts, least, largest):
    def one(position, parts):
        draws = jax.random.uniform(jax.random.fold_in(jax.random.fold_in(own_key, 6), position), (parts,), jnp.float32, least / len(cuts), largest / len(cuts))
        return jnp.repeat(jnp.exp(draws), extent[position] // parts).reshape((-1,) + (1,) * (len(extent) - position - 1))

    loudness = one(*cuts[0])
    for cut in cuts[1:]:
        loudness = loudness * one(*cut)
    return loudness


def gaussian(key, dims, scale, bound, cuts=(), held_as=jnp.bfloat16):
    gain = shard_levels(key, dims, cuts, -0.22, 0.18) if cuts else 1.0
    values = jax.random.normal(key, dims, jnp.float32) * scale * gain
    return jnp.minimum(jnp.maximum(values, -bound), bound).astype(held_as)


def setup_inputs(seed: int = 0) -> dict:
    streams_of = jax.random.split(jax.random.key(seed), 7)
    return {
        "grad_partial": gaussian(streams_of[0], (N_REP, BLOCKS, BS, BS), (1.0 / N_REP ** 0.5), 2.0, ((0, 64), (1, 16))),
        "owner_block": jax.random.permutation(streams_of[1], BLOCKS).astype(jnp.int32),
        "left_stat": draw_left_stat(jax.random.fold_in(streams_of[6], 71), 0),
        "right_stat": draw_right_stat(jax.random.fold_in(streams_of[6], 71), 0),
        "left_root": draw_left_root(jax.random.fold_in(streams_of[6], 71), 0),
        "right_root": draw_right_root(jax.random.fold_in(streams_of[6], 71), 0),
    }


decay_rate = 0.9


def newton_step(stat, root):
    product = stat
    for power in range(5):
        product = jnp.dot(product, root, precision=lax.Precision.HIGHEST, preferred_element_type=jnp.float32)
    return (5.0 * root - product) / 4.0


def reference(grad_partial, owner_block, left_stat, right_stat, left_root, right_root):
    gram_weight = (1.0 - decay_rate) / BS

    def one_slot(items):
        block_id, left_old, right_old, left_guess, right_guess = items
        partials = lax.dynamic_index_in_dim(grad_partial, block_id, 1, keepdims=False)
        grad_block = jnp.sum(partials.astype(jnp.float32), axis=0).astype(jnp.bfloat16)
        left_upd = decay_rate * left_old + gram_weight * jnp.dot(grad_block, grad_block.T, preferred_element_type=jnp.float32)
        right_upd = decay_rate * right_old + gram_weight * jnp.dot(grad_block.T, grad_block, preferred_element_type=jnp.float32)
        left_ref = newton_step(left_upd, left_guess)
        right_ref = newton_step(right_upd, right_guess)
        left_half = jnp.dot(left_ref.astype(jnp.bfloat16), grad_block, preferred_element_type=jnp.float32).astype(jnp.bfloat16)
        result = jnp.dot(left_half, right_ref.astype(jnp.bfloat16), preferred_element_type=jnp.float32).astype(jnp.bfloat16)
        return result, left_upd, right_upd, left_ref, right_ref

    outputs = lax.map(one_slot, (owner_block, left_stat, right_stat, left_root, right_root))
    return outputs[0], outputs[1], outputs[2], outputs[3], outputs[4]
```

```python
import jax
import jax.numpy as jnp
from jax import lax
from jax.sharding import Mesh, PartitionSpec as P

decay_rate = 0.9
REP = ("zh", "x", "y")
XY = ("x", "y")
FSDP = ("zl", "core")
f32, bf16 = jnp.float32, jnp.bfloat16


def exchange(a, axes):
    return lax.all_to_all(a, axes, split_axis=0, concat_axis=0, tiled=True)


def dot32(a, b):
    return jnp.dot(a, b, precision=lax.Precision.HIGHEST, preferred_element_type=f32)


def fifth_power(root):
    square = dot32(root, root)
    return dot32(dot32(square, square), root)


def summed_block(grad_partial, owner_block, ready):
    pieces = grad_partial[0].reshape(4, 16, 32, 512).transpose(1, 0, 2, 3)
    arrived, ready = lax.optimization_barrier((exchange(pieces, XY), ready))
    part = arrived.astype(f32).sum(0).astype(bf16)
    tiles = part.reshape(4, 4, 8, 4, 128).transpose(1, 3, 0, 2, 4).reshape(16, 4, 8, 128)
    by_block = exchange(tiles, FSDP).reshape(64, 8, 128)
    by_slot = jnp.take(by_block, owner_block, axis=0, mode="clip")
    parts = exchange(by_slot, REP).reshape(4, 16, 8, 128)
    mine = parts.astype(f32).sum(0).astype(bf16)
    own = exchange(jnp.broadcast_to(mine[None], (8, 16, 8, 128)), "zl")
    other = lax.ppermute(own, "core", [(0, 1), (1, 0)])
    first = lax.axis_index("core") == 0
    even, odd = jnp.where(first, own, other), jnp.where(first, other, own)
    tiles = jnp.stack([even, odd], axis=1).reshape(4, 4, 16, 8, 128)
    return tiles.transpose(2, 0, 3, 1, 4).reshape(512, 512), ready


def per_device(grad_partial, owner_block, left_stat, right_stat, left_root, right_root):
    gram_weight = (1.0 - decay_rate) / 512
    fifths = (fifth_power(left_root[0]), fifth_power(right_root[0]))
    block, (left_fifth, right_fifth) = summed_block(grad_partial, owner_block, fifths)
    start = (lax.axis_index("zl") * 2 + lax.axis_index("core")) * 32

    def rows(a):
        return lax.dynamic_slice_in_dim(a, start, 32, 0)

    left_new = decay_rate * left_stat[0] + gram_weight * lax.dot_general(
        rows(block), block, (((1,), (1,)), ((), ())), preferred_element_type=f32
    )
    left_next = (5.0 * rows(left_root[0]) - dot32(left_new, left_fifth)) / 4.0
    right_full = decay_rate * right_stat[0] + gram_weight * lax.dot_general(
        block, block, (((0,), (0,)), ((), ())), preferred_element_type=f32
    )
    right_next_full = (5.0 * right_root[0] - dot32(right_full, right_fifth)) / 4.0
    left_half = jnp.dot(left_next.astype(bf16), block, preferred_element_type=f32).astype(bf16)
    result = jnp.dot(left_half, right_next_full.astype(bf16), preferred_element_type=f32).astype(bf16)
    return (result[None], left_new[None], rows(right_full)[None], left_next[None], rows(right_next_full)[None])


def solution(mesh):
    fine = Mesh(mesh.devices.reshape(4, 4, 4, 8, 2), REP + FSDP)
    in_specs = (
        P(REP, FSDP, None, None),
        P(),
        P(REP, FSDP, None),
        P(REP, None, None),
        P(REP, None, None),
        P(REP, None, None),
    )
    return jax.shard_map(
        per_device, mesh=fine, in_specs=in_specs, out_specs=(P(REP, FSDP, None),) * 5, check_vma=False
    )
```

```python
import jax
import jax.numpy as jnp
from jax import lax
from jax.experimental import pallas as pl
from jax.experimental.pallas import tpu as pltpu
from jax.sharding import Mesh, PartitionSpec as P

decay_rate = 0.9
REP = ("zh", "x", "y")
XY = ("x", "y")
FSDP = ("zl", "core")
f32, bf16 = jnp.float32, jnp.bfloat16
VMEM = pl.BlockSpec(memory_space=pltpu.VMEM)
SMEM = pl.BlockSpec(memory_space=pltpu.SMEM)
HBM = pl.BlockSpec(memory_space=pltpu.HBM)


def exchange(a, axes):
    return lax.all_to_all(a, axes, split_axis=0, concat_axis=0, tiled=True)


def dot(a, b, contract=((1,), (0,))):
    return lax.dot_general(a, b, (contract, ((), ())), preferred_element_type=f32)


def halves(a):
    high = a.astype(bf16)
    return high, (a - high.astype(f32)).astype(bf16)


def dot3(a, b):
    return dot(a[0], b[0]) + (dot(a[0], b[1]) + dot(a[1], b[0]))


def regroup_kernel(blocks, pieces):
    for q in range(4):
        pieces[:, q] = blocks[q]


def regroup(blocks):
    return pl.pallas_call(
        regroup_kernel,
        out_shape=jax.ShapeDtypeStruct((16, 4, 32, 512), bf16),
        in_specs=[VMEM],
        out_specs=VMEM,
        compiler_params=pltpu.CompilerParams(vmem_limit_bytes=6 * 2**20),
        name="regroup",
    )(blocks)


def sum_kernel(arrived, tiles):
    for q in range(4):
        total = arrived[0, q].astype(f32)
        for source in range(1, 16):
            total = total + arrived[source, q].astype(f32)
        for piece in range(16):
            row, column = piece // 4 * 8, piece % 4 * 128
            tiles[piece, q] = total[row : row + 8, column : column + 128].astype(bf16)


def sum_to_tiles(arrived):
    return pl.pallas_call(
        sum_kernel,
        out_shape=jax.ShapeDtypeStruct((16, 4, 8, 128), bf16),
        in_specs=[VMEM],
        out_specs=VMEM,
        compiler_params=pltpu.CompilerParams(vmem_limit_bytes=8 * 2**20),
        name="sum_to_tiles",
    )(arrived)


def powers_kernel(left_root, right_root, powers):
    for side, root in enumerate((left_root, right_root)):
        first = halves(root[...])
        square = halves(dot3(first, first))
        fourth = halves(dot3(square, square))
        powers[2 * side], powers[2 * side + 1] = halves(dot3(fourth, first))


def fifth_powers(left_root, right_root):
    return pl.pallas_call(
        powers_kernel,
        out_shape=jax.ShapeDtypeStruct((4, 512, 512), bf16),
        in_specs=[VMEM] * 2,
        out_specs=VMEM,
        compiler_params=pltpu.CompilerParams(vmem_limit_bytes=10 * 2**20),
        cost_estimate=pl.CostEstimate(flops=18 * 2 * 512**3, bytes_accessed=4 * 2**20, transcendentals=0),
        name="fifth_powers",
    )(left_root, right_root)


def tail_kernel(
    place, own, left_stat, left_rows, right_stat, right_root, other_hbm, powers_hbm,
    result, left_new, right_new, left_next, right_next, other, powers, grid, full, sems,
):
    pairs = ((other_hbm, other), (powers_hbm, powers))
    copies = [pltpu.make_async_copy(*pair, sems.at[i]) for i, pair in enumerate(pairs)]
    for copy in copies:
        copy.start()
    core, mine = place[0], place[1]
    gram_weight = (1.0 - decay_rate) / 512
    for tiles, parity in ((own, core), (other, 1 - core)):
        if tiles is other:
            copies[0].wait()
        for chip in range(8):
            column = pl.multiple_of((chip % 2 * 2 + parity) * 128, 128)
            grid[:, pl.ds(chip // 2 * 8, 8), pl.ds(column, 128)] = tiles[chip].astype(f32)
    block = grid[...].reshape(512, 512).astype(bf16)
    stat = decay_rate * right_stat[...] + gram_weight * dot(block, block, ((0,), (0,)))
    full[...] = stat
    rows = grid[mine].astype(bf16)
    stat_rows = decay_rate * left_stat[...] + gram_weight * dot(rows, block, ((1,), (1,)))
    left_new[...] = stat_rows
    copies[1].wait()
    product = dot3(halves(stat_rows), (powers[0], powers[1]))
    next_rows = (5.0 * left_rows[...] - product) / 4.0
    left_next[...] = next_rows
    left_half = dot(next_rows.astype(bf16), block).astype(bf16)
    start = pl.multiple_of(mine * 32, 32)
    right_new[...] = full[pl.ds(start, 32)]
    root = (5.0 * right_root[...] - dot3(halves(stat), (powers[2], powers[3]))) / 4.0
    full[...] = root
    right_next[...] = full[pl.ds(start, 32)]
    result[...] = dot(left_half, root.astype(bf16)).astype(bf16)


def tail(place, *operands):
    rows, whole = (32, 512), (512, 512)
    return pl.pallas_call(
        tail_kernel,
        out_shape=(jax.ShapeDtypeStruct(rows, bf16),) + (jax.ShapeDtypeStruct(rows, f32),) * 4,
        in_specs=[SMEM] + [VMEM] * 5 + [HBM] * 2,
        out_specs=(VMEM,) * 5,
        scratch_shapes=[
            pltpu.VMEM((8, 16, 8, 128), bf16), pltpu.VMEM((4, 512, 512), bf16),
            pltpu.VMEM((16, 32, 512), f32), pltpu.VMEM(whole, f32), pltpu.SemaphoreType.DMA((2,)),
        ],
        compiler_params=pltpu.CompilerParams(vmem_limit_bytes=14 * 2**20),
        name="tail",
    )(place, *operands)


def held(*arrays):
    return lax.optimization_barrier(arrays)


def gathered_tiles(grad_partial, owner_block, left_root, right_root):
    pieces = regroup(grad_partial.reshape(4, 16, 32, 512))
    arrived = exchange(pieces.reshape(16, 128, 512), XY)
    arrived, owner_block, left_root, right_root = held(arrived, owner_block, left_root, right_root)
    by_block = exchange(sum_to_tiles(arrived.reshape(16, 4, 32, 512)), FSDP).reshape(64, 8, 128)
    by_block, owner_block = held(by_block, owner_block)
    by_slot = jnp.take(by_block, owner_block, axis=0, mode="clip")
    by_slot, left_root, right_root = held(by_slot, left_root, right_root)
    powers = fifth_powers(left_root, right_root)
    parts, powers = held(exchange(by_slot, REP), powers)
    mine = parts.reshape(4, 16, 8, 128).astype(f32).sum(0).astype(bf16)
    own = exchange(jnp.broadcast_to(mine[None], (8, 16, 8, 128)), "zl")
    return own, lax.ppermute(own, "core", [(0, 1), (1, 0)]), powers


def per_device(grad_partial, owner_block, left_stat, right_stat, left_root, right_root):
    own, other, powers = gathered_tiles(grad_partial, owner_block, left_root[0], right_root[0])
    core = lax.axis_index("core")
    mine = lax.axis_index("zl") * 2 + core
    left_rows = lax.dynamic_slice_in_dim(left_root[0], mine * 32, 32, 0)
    outs = tail(
        jnp.stack([core, mine]).astype(jnp.int32), own, left_stat[0], left_rows,
        right_stat[0], right_root[0], other, powers,
    )
    return tuple(out[None] for out in outs)


def solution(mesh):
    fine = Mesh(mesh.devices.reshape(4, 4, 4, 8, 2), REP + FSDP)
    in_specs = (
        P(REP, FSDP, None, None),
        P(),
        P(REP, FSDP, None),
        P(REP, None, None),
        P(REP, None, None),
        P(REP, None, None),
    )
    return jax.shard_map(
        per_device, mesh=fine, in_specs=in_specs, out_specs=(P(REP, FSDP, None),) * 5, check_vma=False
    )
```

```python
import jax
import jax.numpy as jnp
from jax import lax
from jax.experimental import pallas as pl
from jax.experimental.pallas import tpu as pltpu
from jax.sharding import Mesh, PartitionSpec as P

decay_rate = 0.9
REP = ("zh", "x", "y")
FSDP = ("zl", "core")
f32, bf16 = jnp.float32, jnp.bfloat16
VMEM = pl.BlockSpec(memory_space=pltpu.VMEM)
SMEM = pl.BlockSpec(memory_space=pltpu.SMEM)
HBM = pl.BlockSpec(memory_space=pltpu.HBM)


PLANE = ("x", "y", "core")
ALONG_X = [[[(x * 4 + y) * 2 + core for x in range(4)] for y in range(4)] for core in range(2)]
ALONG_Y = [[[(x * 4 + y) * 2 + core for y in range(4)] for x in range(4)] for core in range(2)]
FIRST, SECOND = ALONG_X[0] + ALONG_Y[1], ALONG_Y[0] + ALONG_X[1]


def exchange(a, axes, groups=None):
    return lax.all_to_all(a, axes, split_axis=0, concat_axis=0, axis_index_groups=groups, tiled=True)


def dot(a, b, contract=((1,), (0,))):
    return lax.dot_general(a, b, (contract, ((), ())), preferred_element_type=f32)


def halves(a):
    high = a.astype(bf16)
    return high, (a - high.astype(f32)).astype(bf16)


def dot3(a, b):
    return dot(a[0], b[0]) + (dot(a[0], b[1]) + dot(a[1], b[0]))


def regroup_kernel(place, blocks, pieces):
    def copy(along_x):
        for near in range(4):
            for far in range(4):
                for q in range(4):
                    pieces[near, far, q] = blocks[q, 4 * near + far if along_x else 4 * far + near]

    pl.when(place[0] == 0)(lambda: copy(True))
    pl.when(place[0] != 0)(lambda: copy(False))


def regroup(place, blocks):
    return pl.pallas_call(
        regroup_kernel,
        out_shape=jax.ShapeDtypeStruct((4, 4, 4, 32, 512), bf16),
        in_specs=[SMEM, VMEM],
        out_specs=VMEM,
        compiler_params=pltpu.CompilerParams(vmem_limit_bytes=6 * 2**20),
        name="regroup",
    )(place, blocks)


def first_sum_kernel(arrived, sums):
    for far in range(4):
        for q in range(4):
            total = arrived[0, far, q].astype(f32)
            for source in range(1, 4):
                total = total + arrived[source, far, q].astype(f32)
            sums[far, q] = total.astype(bf16)


def first_sum(arrived):
    return pl.pallas_call(
        first_sum_kernel,
        out_shape=jax.ShapeDtypeStruct((4, 4, 32, 512), bf16),
        in_specs=[VMEM],
        out_specs=VMEM,
        compiler_params=pltpu.CompilerParams(vmem_limit_bytes=4 * 2**20),
        name="first_sum",
    )(arrived)


def second_sum_kernel(arrived, tiles):
    for q in range(4):
        total = arrived[0, q].astype(f32)
        for source in range(1, 4):
            total = total + arrived[source, q].astype(f32)
        for piece in range(16):
            row, column = piece // 4 * 8, piece % 4 * 128
            tiles[piece, q] = total[row : row + 8, column : column + 128].astype(bf16)


def second_sum(arrived):
    return pl.pallas_call(
        second_sum_kernel,
        out_shape=jax.ShapeDtypeStruct((16, 4, 8, 128), bf16),
        in_specs=[VMEM],
        out_specs=VMEM,
        compiler_params=pltpu.CompilerParams(vmem_limit_bytes=4 * 2**20),
        name="second_sum",
    )(arrived)


def ahead_kernel(place, left_stat, right_stat, left_root, right_root, powers, left_base, right_base, right_old):
    start = pl.multiple_of(place[1] * 32, 32)
    for side, root in enumerate((left_root, right_root)):
        first = halves(root[...])
        square = halves(dot3(first, first))
        fourth = halves(dot3(square, square))
        powers[2 * side], powers[2 * side + 1] = halves(dot3(fourth, first))
    kept = dot3(halves(left_stat[...]), (powers[0], powers[1]))
    left_base[...] = (5.0 * left_root[pl.ds(start, 32)] - decay_rate * kept) / 4.0
    kept = dot3(halves(right_stat[...]), (powers[2], powers[3]))
    right_base[...] = (5.0 * right_root[...] - decay_rate * kept) / 4.0
    right_old[...] = decay_rate * right_stat[pl.ds(start, 32)]


def ahead(place, left_stat, right_stat, left_root, right_root):
    shapes = ((4, 512, 512), bf16), ((32, 512), f32), ((512, 512), f32), ((32, 512), f32)
    return pl.pallas_call(
        ahead_kernel,
        out_shape=tuple(jax.ShapeDtypeStruct(*shape) for shape in shapes),
        in_specs=[SMEM] + [VMEM] * 4,
        out_specs=(VMEM,) * 4,
        compiler_params=pltpu.CompilerParams(vmem_limit_bytes=12 * 2**20),
        cost_estimate=pl.CostEstimate(flops=22 * 2 * 512**3, bytes_accessed=6 * 2**20, transcendentals=0),
        name="ahead",
    )(place, left_stat, right_stat, left_root, right_root)


def tail_kernel(
    place, own, left_stat, powers, left_base, right_base, right_old, other_hbm,
    result, left_new, right_new, left_next, right_next, other, grid, full, sem,
):
    copy = pltpu.make_async_copy(other_hbm, other, sem)
    copy.start()
    core, mine = place[0], place[1]
    start = pl.multiple_of(mine * 32, 32)
    gram_weight = (1.0 - decay_rate) / 512
    for tiles, parity in ((own, core), (other, 1 - core)):
        if tiles is other:
            copy.wait()
        for chip in range(8):
            column = pl.multiple_of((chip % 2 * 2 + parity) * 128, 128)
            grid[:, pl.ds(chip // 2 * 8, 8), pl.ds(column, 128)] = tiles[:, chip].astype(f32)
    block = grid[...].reshape(512, 512).astype(bf16)
    rows = grid[mine].astype(bf16)
    gram_rows = gram_weight * dot(rows, block, ((1,), (1,)))
    gram = gram_weight * dot(block, block, ((0,), (0,)))
    full[...] = gram
    left_new[...] = decay_rate * left_stat[...] + gram_rows
    next_rows = left_base[...] - 0.25 * dot3(halves(gram_rows), (powers[0], powers[1]))
    left_next[...] = next_rows
    left_half = dot(next_rows.astype(bf16), block).astype(bf16)
    right_new[...] = right_old[...] + full[pl.ds(start, 32)]
    root = right_base[...] - 0.25 * dot3(halves(gram), (powers[2], powers[3]))
    full[...] = root
    right_next[...] = full[pl.ds(start, 32)]
    result[...] = dot(left_half, root.astype(bf16)).astype(bf16)


def tail(place, *operands):
    rows, whole = (32, 512), (512, 512)
    return pl.pallas_call(
        tail_kernel,
        out_shape=(jax.ShapeDtypeStruct(rows, bf16),) + (jax.ShapeDtypeStruct(rows, f32),) * 4,
        in_specs=[SMEM] + [VMEM] * 6 + [HBM],
        out_specs=(VMEM,) * 5,
        scratch_shapes=[
            pltpu.VMEM((16, 8, 8, 128), bf16), pltpu.VMEM((16, 32, 512), f32), pltpu.VMEM(whole, f32), pltpu.SemaphoreType.DMA,
        ],
        compiler_params=pltpu.CompilerParams(vmem_limit_bytes=12 * 2**20),
        name="tail",
    )(place, *operands)


def held(*arrays):
    return lax.optimization_barrier(arrays)


def per_device(grad_partial, owner_block, left_stat, right_stat, left_root, right_root):
    core = lax.axis_index("core")
    place = jnp.stack([core, lax.axis_index("zl") * 2 + core]).astype(jnp.int32)
    pieces = regroup(place, grad_partial.reshape(4, 16, 32, 512))
    sums = first_sum(exchange(pieces, PLANE, FIRST))
    tiles = second_sum(exchange(sums, PLANE, SECOND))
    by_block, owner_block = held(exchange(tiles, FSDP), owner_block)
    by_slot = jnp.take(by_block.reshape(64, 8, 128), owner_block, axis=0, mode="clip")
    by_slot, *slot = held(by_slot, left_stat[0], right_stat[0], left_root[0], right_root[0])
    parts, *ready = held(exchange(by_slot.reshape(4, 16, 8, 128), "zh"), *ahead(place, *slot))
    mine = parts.astype(f32).sum(0).astype(bf16)
    spread = jnp.broadcast_to(mine[:, None], (16, 8, 8, 128)).reshape(128, 8, 128)
    own = exchange(spread, ("x", "y", "zl")).reshape(16, 8, 8, 128)
    other = lax.ppermute(own, "core", [(0, 1), (1, 0)])
    outs = tail(place, own, left_stat[0], *ready, other)
    return tuple(out[None] for out in outs)


def solution(mesh):
    fine = Mesh(mesh.devices.reshape(4, 4, 4, 8, 2), REP + FSDP)
    in_specs = (
        P(REP, FSDP, None, None),
        P(),
        P(REP, FSDP, None),
        P(REP, None, None),
        P(REP, None, None),
        P(REP, None, None),
    )
    return jax.shard_map(
        per_device, mesh=fine, in_specs=in_specs, out_specs=(P(REP, FSDP, None),) * 5, check_vma=False
    )
```

```python
import jax
import jax.numpy as jnp
from jax import lax
from jax.experimental import pallas as pl
from jax.experimental.pallas import tpu as pltpu
from jax.sharding import Mesh, PartitionSpec as P

decay_rate = 0.9
REP = ("zh", "x", "y")
FSDP = ("zl", "core")
f32, bf16 = jnp.float32, jnp.bfloat16
VMEM = pl.BlockSpec(memory_space=pltpu.VMEM)
SMEM = pl.BlockSpec(memory_space=pltpu.SMEM)
HBM = pl.BlockSpec(memory_space=pltpu.HBM)


PLANE = ("x", "y", "core")
EVEN, ODD = ((0, 1), (2, 3)), ((1, 2), (3, 0))
PLACES = (((0, 1, 1, 0), (1, 0, 1, 0)), ((0, 0, 1, 1), (0, 1, 0, 1)))


def squares(pairs, places, core):
    chips = [[(x, y) for x in xs for y in ys] for xs in pairs for ys in pairs]
    ordered = [sorted(square, key=lambda chip: 2 * places[chip[0]] + places[chip[1]]) for square in chips]
    return [[(x * 4 + y) * 2 + core for x, y in square] for square in ordered]


FIRST = squares(EVEN, PLACES[0][0], 0) + squares(ODD, PLACES[1][0], 1)
SECOND = squares(ODD, PLACES[0][1], 0) + squares(EVEN, PLACES[1][1], 1)


def exchange(a, axes, groups=None):
    return lax.all_to_all(a, axes, split_axis=0, concat_axis=0, axis_index_groups=groups, tiled=True)


def dot(a, b, contract=((1,), (0,))):
    return lax.dot_general(a, b, (contract, ((), ())), preferred_element_type=f32)


def halves(a):
    high = a.astype(bf16)
    return high, (a - high.astype(f32)).astype(bf16)


def dot3(a, b):
    return dot(a[0], b[0]) + (dot(a[0], b[1]) + dot(a[1], b[0]))


def regroup_kernel(place, blocks, pieces):
    def copy(first, second):
        for x in range(4):
            for y in range(4):
                near, far = 2 * first[x] + first[y], 2 * second[x] + second[y]
                for q in range(4):
                    pieces[near, far, q] = blocks[q, 4 * x + y]

    pl.when(place[0] == 0)(lambda: copy(*PLACES[0]))
    pl.when(place[0] != 0)(lambda: copy(*PLACES[1]))


def regroup(place, blocks):
    return pl.pallas_call(
        regroup_kernel,
        out_shape=jax.ShapeDtypeStruct((4, 4, 4, 32, 512), bf16),
        in_specs=[SMEM, VMEM],
        out_specs=VMEM,
        compiler_params=pltpu.CompilerParams(vmem_limit_bytes=6 * 2**20),
        name="regroup",
    )(place, blocks)


def first_sum_kernel(arrived, sums):
    for far in range(4):
        for q in range(4):
            total = arrived[0, far, q].astype(f32)
            for source in range(1, 4):
                total = total + arrived[source, far, q].astype(f32)
            sums[far, q] = total.astype(bf16)


def first_sum(arrived):
    return pl.pallas_call(
        first_sum_kernel,
        out_shape=jax.ShapeDtypeStruct((4, 4, 32, 512), bf16),
        in_specs=[VMEM],
        out_specs=VMEM,
        compiler_params=pltpu.CompilerParams(vmem_limit_bytes=4 * 2**20),
        name="first_sum",
    )(arrived)


def second_sum_kernel(arrived, tiles):
    for q in range(4):
        total = arrived[0, q].astype(f32)
        for source in range(1, 4):
            total = total + arrived[source, q].astype(f32)
        for piece in range(16):
            row, column = piece // 4 * 8, piece % 4 * 128
            tiles[piece, q] = total[row : row + 8, column : column + 128].astype(bf16)


def second_sum(arrived):
    return pl.pallas_call(
        second_sum_kernel,
        out_shape=jax.ShapeDtypeStruct((16, 4, 8, 128), bf16),
        in_specs=[VMEM],
        out_specs=VMEM,
        compiler_params=pltpu.CompilerParams(vmem_limit_bytes=4 * 2**20),
        name="second_sum",
    )(arrived)


def ahead_kernel(place, left_stat, right_stat, left_root, right_root, powers, left_base, right_base, right_old):
    start = pl.multiple_of(place[1] * 32, 32)
    for side, root in enumerate((left_root, right_root)):
        first = halves(root[...])
        square = halves(dot3(first, first))
        fourth = halves(dot3(square, square))
        powers[2 * side], powers[2 * side + 1] = halves(dot3(fourth, first))
    kept = dot3(halves(left_stat[...]), (powers[0], powers[1]))
    left_base[...] = (5.0 * left_root[pl.ds(start, 32)] - decay_rate * kept) / 4.0
    kept = dot3(halves(right_stat[...]), (powers[2], powers[3]))
    right_base[...] = (5.0 * right_root[...] - decay_rate * kept) / 4.0
    right_old[...] = decay_rate * right_stat[pl.ds(start, 32)]


def ahead(place, left_stat, right_stat, left_root, right_root):
    shapes = ((4, 512, 512), bf16), ((32, 512), f32), ((512, 512), f32), ((32, 512), f32)
    return pl.pallas_call(
        ahead_kernel,
        out_shape=tuple(jax.ShapeDtypeStruct(*shape) for shape in shapes),
        in_specs=[SMEM] + [VMEM] * 4,
        out_specs=(VMEM,) * 4,
        compiler_params=pltpu.CompilerParams(vmem_limit_bytes=12 * 2**20),
        cost_estimate=pl.CostEstimate(flops=22 * 2 * 512**3, bytes_accessed=6 * 2**20, transcendentals=0),
        name="ahead",
    )(place, left_stat, right_stat, left_root, right_root)


def tail_kernel(
    place, own, left_stat, powers, left_base, right_base, right_old, other_hbm,
    result, left_new, right_new, left_next, right_next, other, grid, full, sem,
):
    copy = pltpu.make_async_copy(other_hbm, other, sem)
    copy.start()
    core, mine = place[0], place[1]
    start = pl.multiple_of(mine * 32, 32)
    gram_weight = (1.0 - decay_rate) / 512
    for tiles, parity in ((own, core), (other, 1 - core)):
        if tiles is other:
            copy.wait()
        for chip in range(8):
            column = pl.multiple_of((chip % 2 * 2 + parity) * 128, 128)
            grid[:, pl.ds(chip // 2 * 8, 8), pl.ds(column, 128)] = tiles[:, chip].astype(f32)
    block = grid[...].reshape(512, 512).astype(bf16)
    rows = grid[mine].astype(bf16)
    gram_rows = gram_weight * dot(rows, block, ((1,), (1,)))
    gram = gram_weight * dot(block, block, ((0,), (0,)))
    full[...] = gram
    left_new[...] = decay_rate * left_stat[...] + gram_rows
    next_rows = left_base[...] - 0.25 * dot3(halves(gram_rows), (powers[0], powers[1]))
    left_next[...] = next_rows
    left_half = dot(next_rows.astype(bf16), block).astype(bf16)
    right_new[...] = right_old[...] + full[pl.ds(start, 32)]
    root = right_base[...] - 0.25 * dot3(halves(gram), (powers[2], powers[3]))
    full[...] = root
    right_next[...] = full[pl.ds(start, 32)]
    result[...] = dot(left_half, root.astype(bf16)).astype(bf16)


def tail(place, *operands):
    rows, whole = (32, 512), (512, 512)
    return pl.pallas_call(
        tail_kernel,
        out_shape=(jax.ShapeDtypeStruct(rows, bf16),) + (jax.ShapeDtypeStruct(rows, f32),) * 4,
        in_specs=[SMEM] + [VMEM] * 6 + [HBM],
        out_specs=(VMEM,) * 5,
        scratch_shapes=[
            pltpu.VMEM((16, 8, 8, 128), bf16), pltpu.VMEM((16, 32, 512), f32), pltpu.VMEM(whole, f32), pltpu.SemaphoreType.DMA,
        ],
        compiler_params=pltpu.CompilerParams(vmem_limit_bytes=12 * 2**20),
        name="tail",
    )(place, *operands)


def held(*arrays):
    return lax.optimization_barrier(arrays)


def per_device(grad_partial, owner_block, left_stat, right_stat, left_root, right_root):
    core = lax.axis_index("core")
    place = jnp.stack([core, lax.axis_index("zl") * 2 + core]).astype(jnp.int32)
    pieces = regroup(place, grad_partial.reshape(4, 16, 32, 512))
    sums = first_sum(exchange(pieces, PLANE, FIRST))
    tiles = second_sum(exchange(sums, PLANE, SECOND))
    by_block, owner_block = held(exchange(tiles, FSDP), owner_block)
    by_slot = jnp.take(by_block.reshape(64, 8, 128), owner_block, axis=0, mode="clip")
    by_slot, *slot = held(by_slot, left_stat[0], right_stat[0], left_root[0], right_root[0])
    parts, *ready = held(exchange(by_slot.reshape(4, 16, 8, 128), "zh"), *ahead(place, *slot))
    mine = parts.astype(f32).sum(0).astype(bf16)
    spread = jnp.broadcast_to(mine[:, None], (16, 8, 8, 128)).reshape(128, 8, 128)
    own = exchange(spread, ("x", "y", "zl")).reshape(16, 8, 8, 128)
    other = lax.ppermute(own, "core", [(0, 1), (1, 0)])
    outs = tail(place, own, left_stat[0], *ready, other)
    return tuple(out[None] for out in outs)


def solution(mesh):
    fine = Mesh(mesh.devices.reshape(4, 4, 4, 8, 2), REP + FSDP)
    in_specs = (
        P(REP, FSDP, None, None),
        P(),
        P(REP, FSDP, None),
        P(REP, None, None),
        P(REP, None, None),
        P(REP, None, None),
    )
    return jax.shard_map(
        per_device, mesh=fine, in_specs=in_specs, out_specs=(P(REP, FSDP, None),) * 5, check_vma=False
    )
```
